512 devices in a mesh: depth: 128 (over z, x, core), head: 4 (over y).
Axes of the slice: x: 4, y: 4, z: 16, core: 2. Of those that a mesh axis runs over, the one named last changes fastest.
Arguments:
- queries: bfloat16 [1536, 768, 256], P('depth', 'head'), may hold values from -8 to 8
- keys: bfloat16 [1536, 768, 256], P('depth', 'head'), may hold values from -6 to 6
- values: bfloat16 [1536, 768, 256], P('depth', 'head'), may hold values from -6 to 6
- w_out: bfloat16 [768, 768], P('head'), may hold values from -0.21875 to 0.21875
Outputs:
- mixed: bfloat16 [1536, 768, 256], P('depth', 'head')
The draws below stay inside these ranges and needn't reach their ends.
All inputs are finite; a program needn't handle non-finite values.
Results may differ from the reference program's by a relative error of at most 0.0057.
Values may be sent and summed in bfloat16 or wider, within the bound.
A program may use at most 64 MiB of HBM per device.

```python
import math
import jax
import jax.numpy as jnp
from jax import lax

HEADS = 12
HEAD_DIM = 64
WIDTH = 768
COLS = 256
ROWS = 1536


def key_field(key):
    return jnp.clip(jax.random.normal(key, (ROWS, WIDTH, COLS), jnp.float32), -6.0, 6.0)


def draw_keys(key, part):
    base = key_field(key)
    return base.astype(jnp.bfloat16)


def draw_queries(key, part):
    key = jax.random.fold_in(key, 23)
    fresh = jnp.clip(jax.random.normal(key, (ROWS, WIDTH, COLS), jnp.float32), -6.0, 6.0)
    return fresh.astype(jnp.bfloat16)


def steps_of(rng, dims, pieces, low, largest):
    gain, own = 1.0, jax.random.fold_in(rng, 6)
    for position, shards_of in pieces:
        steps = jnp.exp(jax.random.uniform(jax.random.fold_in(own, position), (shards_of,), jnp.float32, low / len(pieces), largest / len(pieces)))
        gain = gain * jnp.repeat(steps, dims[position] // shards_of).reshape([-1 if axis == position else 1 for axis in range(len(dims))])
    return gain


def noise(rng, dims, width, limit, pieces=(), kind=jnp.bfloat16):
    values = width * jax.random.normal(rng, dims, jnp.float32)
    if pieces:
        values = values * steps_of(rng, dims, pieces, -0.22, 0.18)
    return jnp.clip(values, -limit, limit).astype(kind)


def setup_inputs(seed: int = 0) -> dict:
    streams_of = jax.random.split(jax.random.key(seed), 5)
    queries = draw_queries(jax.random.fold_in(streams_of[4], 71), 0)
    keys = draw_keys(jax.random.fold_in(streams_of[4], 71), 0)
    values = noise(streams_of[2], (ROWS, WIDTH, COLS), 1.0, 6.0, ((0, 128), (1, 4)))
    w_out = noise(streams_of[3], (WIDTH, WIDTH), WIDTH ** -0.5, 0.21875, ((0, 4),))
    return dict(queries=queries, keys=keys, values=values, w_out=w_out)


def reference(queries, keys, values, w_out):
    scaling = 1.0 / math.sqrt(HEAD_DIM * ROWS)
    query_heads = queries.reshape(ROWS, HEADS, HEAD_DIM, COLS)
    key_heads = keys.reshape(ROWS, HEADS, HEAD_DIM, COLS)
    value_heads = values.reshape(ROWS, HEADS, HEAD_DIM, COLS)

    def one_head(number):
        query_part = lax.dynamic_index_in_dim(query_heads, number, 1, keepdims=False).astype(jnp.float32)
        key_part = lax.dynamic_index_in_dim(key_heads, number, 1, keepdims=False).astype(jnp.float32)
        value_part = lax.dynamic_index_in_dim(value_heads, number, 1, keepdims=False).astype(jnp.float32)
        logits = jnp.einsum('rei,rej->ij', query_part, key_part)
        probs = jax.nn.softmax(logits * scaling, axis=-1).astype(jnp.bfloat16)
        attended = jnp.einsum('ij,rej->rei', probs.astype(jnp.float32), value_part)
        return attended.astype(jnp.bfloat16)
    heads_out = lax.map(one_head, jnp.arange(HEADS, dtype=jnp.int32))
    attended = jnp.transpose(heads_out, (1, 0, 2, 3)).reshape(ROWS, WIDTH, COLS)

    def one_row(row_block):
        return jnp.dot(w_out, row_block, preferred_element_type=jnp.float32).astype(jnp.bfloat16)
    return lax.map(one_row, attended)
```

```python
import math

import jax
import jax.numpy as jnp
from jax import lax
from jax.experimental import pallas as pl
from jax.experimental.pallas import tpu as pltpu
from jax.sharding import PartitionSpec as P

HEAD_DIM = 64
NZ, NX, NY, NC = 16, 4, 4, 2
LOCAL_HEADS = 3
ROWS_HERE = 12
WIDTH_HERE = LOCAL_HEADS * HEAD_DIM
COLS = 256
HALF = COLS // NC
XROWS = HALF // NX
GROUPS = XROWS // 8
HALF_SEQ = ROWS_HERE // 2
SCALING = 1.0 / math.sqrt(HEAD_DIM * ROWS_HERE * NZ * NX * NC)
MESH = pl.DeviceIdType.MESH


def kernel(
    q_hbm, k_hbm, v_hbm, w_hbm, out_hbm,
    q_v, k_v, vals, w_v, part, c_recv, csum, x_recv, xsum, z_recv, pg, zg, probs, att, out_v,
    load_sem, v_ssem, v_rsem, c_ssem, c_rsem, x_ssem, x_rsem, z_ssem, z_rsem,
    y_ssem, y_rsem, zg_ssem, zg_rsem, xg_ssem, xg_rsem, cg_ssem, cg_rsem, out_sem,
):
    me = lax.axis_index("depth")
    y = lax.axis_index("head")
    core = lax.rem(me, NC)
    x = lax.rem(me // NC, NX)
    z = me // (NC * NX)

    def at(z=z, x=x, core=core, y=y):
        return ((z * NX + x) * NC + core, y)

    def turn(index, by, size):
        return lax.rem(index + by, size)

    def send(src, dst, ssem, rsem, device):
        copy = pltpu.make_async_remote_copy(
            src_ref=src, dst_ref=dst, send_sem=ssem, recv_sem=rsem,
            device_id=device, device_id_type=MESH,
        )
        copy.start()
        return copy

    def arrived(dst, sem):
        pltpu.make_async_remote_copy(
            src_ref=dst, dst_ref=dst, send_sem=sem, recv_sem=sem,
            device_id=at(), device_id_type=MESH,
        ).wait_recv()

    mate = at(core=1 - core)
    barrier = pltpu.get_barrier_semaphore()
    partners = (
        [at(y=turn(y, d, NY)) for d in range(1, NY)]
        + [mate]
        + [at(x=turn(x, d, NX)) for d in range(1, NX)]
        + [at(z=turn(z, d, NZ)) for d in range(1, NZ)]
    )
    for partner in partners:
        pl.semaphore_signal(barrier, inc=1, device_id=partner, device_id_type=MESH)

    loads = []
    for h in range(LOCAL_HEADS):
        features = pl.ds(h * HEAD_DIM, HEAD_DIM)
        pair = (
            pltpu.make_async_copy(q_hbm.at[:, features, :], q_v.at[h], load_sem.at[2 * h]),
            pltpu.make_async_copy(k_hbm.at[:, features, :], k_v.at[h], load_sem.at[2 * h + 1]),
        )
        for copy in pair:
            copy.start()
        loads.append(pair)
    load_v = pltpu.make_async_copy(v_hbm, vals.at[y], load_sem.at[2 * LOCAL_HEADS])
    load_v.start()
    load_w = pltpu.make_async_copy(w_hbm, w_v, load_sem.at[2 * LOCAL_HEADS + 1])
    load_w.start()

    started = []

    def partial_logits(h):
        for copy in loads[h]:
            copy.wait()
        part[h] = lax.dot_general(
            q_v[h].reshape(ROWS_HERE * HEAD_DIM, COLS),
            k_v[h].reshape(ROWS_HERE * HEAD_DIM, COLS),
            (((0,), (0,)), ((), ())),
            preferred_element_type=jnp.float32,
        )

    def to_mate(h):
        theirs = pl.ds(pl.multiple_of((1 - core) * HALF, HALF), HALF)
        started.append(send(part.at[h, theirs], c_recv.at[h], c_ssem.at[h], c_rsem.at[h], mate))

    partial_logits(0)
    pl.semaphore_wait(barrier, len(partners))
    to_mate(0)

    left, right, far = turn(y, NY - 1, NY), turn(y, 1, NY), turn(y, 2, NY)
    first, second = pl.ds(0, HALF_SEQ), pl.ds(HALF_SEQ, HALF_SEQ)
    for number, (rows, target) in enumerate(
        ((first, right), (second, left), (second, right), (first, left))
    ):
        started.append(send(
            v_hbm.at[rows], vals.at[y, rows], v_ssem.at[number], v_rsem.at[number], at(y=target)
        ))

    for h in range(1, LOCAL_HEADS):
        partial_logits(h)
        to_mate(h)

    ours = pl.ds(pl.multiple_of(core * HALF, HALF), HALF)
    for h in range(LOCAL_HEADS):
        arrived(c_recv.at[h], c_rsem.at[h])
        csum[h] = (part[h, ours, :] + c_recv[h]).reshape(NX, XROWS, COLS)
        for d in range(1, NX):
            other = turn(x, d, NX)
            started.append(send(
                csum.at[h, other], x_recv.at[h, x], x_ssem.at[h, d], x_rsem.at[h, x], at(x=other)
            ))

    for h in range(LOCAL_HEADS):
        total = csum[h, x]
        for d in range(1, NX):
            other = turn(x, d, NX)
            arrived(x_recv.at[h, other], x_rsem.at[h, other])
            total = total + x_recv[h, other]
        xsum[h] = total.reshape(GROUPS, 8, COLS)
        for t in range(GROUPS):
            owner = lax.rem(t * 4 + h + NZ - 2 * core, NZ)

            @pl.when(owner != z)
            def _():
                send(
                    xsum.at[h, t], z_recv.at[z], z_ssem.at[h, t], z_rsem.at[z], at(z=owner)
                )

            @pl.when(owner == z)
            def _():
                z_recv[z] = xsum[h, t]

    turned = turn(z, 2 * core, NZ)
    own_head, own_group = lax.rem(turned, 4), turned // 4

    @pl.when(own_head < LOCAL_HEADS)
    def _():
        for d in range(1, NZ):
            other = turn(z, d, NZ)
            arrived(z_recv.at[other], z_rsem.at[other])
        logits = jnp.sum(z_recv[...], axis=0) * SCALING
        top = jnp.max(logits, axis=-1, keepdims=True)
        powers = jnp.exp(logits - top)
        p = powers / jnp.sum(powers, axis=-1, keepdims=True)
        pg[y] = jnp.concatenate([p[:, :128], p[:, 128:]], axis=0).astype(jnp.bfloat16)
        copies = [
            send(pg.at[y], pg.at[y], y_ssem.at[d], y_rsem.at[y], at(y=turn(y, d, NY)))
            for d in range(1, NY)
        ]
        for d in range(1, NY):
            other = turn(y, d, NY)
            arrived(pg.at[other], y_rsem.at[other])
        mine = own_head * GROUPS + own_group
        for d in range(1, NZ):
            copies.append(send(
                pg, zg.at[mine], zg_ssem.at[d], zg_rsem.at[mine], at(z=turn(z, d, NZ))
            ))
        zg[mine] = pg[...]
        for copy in copies:
            copy.wait_send()

    arrived(vals.at[left, first], v_rsem.at[0])
    started.append(send(
        vals.at[left, first], vals.at[left, first], v_ssem.at[4], v_rsem.at[4], at(y=right)
    ))
    arrived(vals.at[right, second], v_rsem.at[1])
    started.append(send(
        vals.at[right, second], vals.at[right, second], v_ssem.at[5], v_rsem.at[5], at(y=left)
    ))

    here = core * NX + x
    for h in range(LOCAL_HEADS):
        for t in range(GROUPS):
            number = h * GROUPS + t
            owner = lax.rem(t * 4 + h + NZ - 2 * core, NZ)

            @pl.when(owner != z)
            def _():
                arrived(zg.at[number], zg_rsem.at[number])

        for other_y in range(NY):
            blocks = []
            for t in range(GROUPS):
                block = zg[h * GROUPS + t, other_y].astype(jnp.float32)
                blocks.append(jnp.concatenate([block[:8], block[8:]], axis=1))
            probs[h, other_y, here] = jnp.concatenate(blocks, axis=0).astype(jnp.bfloat16)
        for d in range(1, NX):
            started.append(send(
                probs.at[h, :, here], probs.at[h, :, here],
                xg_ssem.at[h, d], xg_rsem.at[h, x], at(x=turn(x, d, NX)),
            ))

    our_blocks = pl.ds(pl.multiple_of(core * NX, NX), NX)
    mate_blocks = pl.ds(pl.multiple_of((1 - core) * NX, NX), NX)
    for h in range(LOCAL_HEADS):
        for d in range(1, NX):
            other = turn(x, d, NX)
            arrived(probs.at[h, :, core * NX + other], xg_rsem.at[h, other])
        started.append(send(
            probs.at[h, :, our_blocks], probs.at[h, :, our_blocks], cg_ssem.at[h], cg_rsem.at[h], mate
        ))

    load_v.wait()
    load_w.wait()
    arrived(vals.at[right, first], v_rsem.at[3])
    arrived(vals.at[left, second], v_rsem.at[2])
    arrived(vals.at[far, first], v_rsem.at[4])
    arrived(vals.at[far, second], v_rsem.at[5])
    for h in range(LOCAL_HEADS):
        arrived(probs.at[h, :, mate_blocks], cg_rsem.at[h])
        features = pl.ds(h * HEAD_DIM, HEAD_DIM)
        for other_y in range(NY):
            attended = lax.dot_general(
                vals[other_y, :, features, :].reshape(ROWS_HERE * HEAD_DIM, COLS),
                probs[h, other_y].reshape(COLS, COLS),
                (((1,), (1,)), ((), ())),
                preferred_element_type=jnp.float32,
            )
            att[:, pl.ds(other_y * WIDTH_HERE + h * HEAD_DIM, HEAD_DIM), :] = (
                attended.astype(jnp.bfloat16).reshape(ROWS_HERE, HEAD_DIM, COLS)
            )

    for r in range(ROWS_HERE):
        out_v[r] = jnp.dot(w_v[...], att[r], preferred_element_type=jnp.float32).astype(jnp.bfloat16)
        pltpu.make_async_copy(out_v.at[r], out_hbm.at[r], out_sem.at[r]).start()
    for r in range(ROWS_HERE):
        pltpu.make_async_copy(out_v.at[r], out_hbm.at[r], out_sem.at[r]).wait()

    for copy in started:
        copy.wait_send()
    for h in range(LOCAL_HEADS):
        for t in range(GROUPS):
            owner = lax.rem(t * 4 + h + NZ - 2 * core, NZ)

            @pl.when(owner != z)
            def _():
                pltpu.make_async_remote_copy(
                    src_ref=xsum.at[h, t], dst_ref=z_recv.at[z],
                    send_sem=z_ssem.at[h, t], recv_sem=z_rsem.at[z],
                    device_id=at(z=owner), device_id_type=MESH,
                ).wait_send()


def per_device(queries, keys, values, w_out):
    f32, bf16 = jnp.float32, jnp.bfloat16
    dma = pltpu.SemaphoreType.DMA
    whole = WIDTH_HERE * NY
    any_spec = pl.BlockSpec(memory_space=pl.ANY)
    return pl.pallas_call(
        kernel,
        out_shape=jax.ShapeDtypeStruct(values.shape, bf16),
        in_specs=[any_spec] * 4,
        out_specs=any_spec,
        scratch_shapes=[
            pltpu.VMEM((LOCAL_HEADS, ROWS_HERE, HEAD_DIM, COLS), bf16),
            pltpu.VMEM((LOCAL_HEADS, ROWS_HERE, HEAD_DIM, COLS), bf16),
            pltpu.VMEM((NY, ROWS_HERE, WIDTH_HERE, COLS), bf16),
            pltpu.VMEM((WIDTH_HERE, whole), bf16),
            pltpu.VMEM((LOCAL_HEADS, COLS, COLS), f32),
            pltpu.VMEM((LOCAL_HEADS, HALF, COLS), f32),
            pltpu.VMEM((LOCAL_HEADS, NX, XROWS, COLS), f32),
            pltpu.VMEM((LOCAL_HEADS, NX, XROWS, COLS), f32),
            pltpu.VMEM((LOCAL_HEADS, GROUPS, 8, COLS), f32),
            pltpu.VMEM((NZ, 8, COLS), f32),
            pltpu.VMEM((NY, 16, 128), bf16),
            pltpu.VMEM((LOCAL_HEADS * GROUPS, NY, 16, 128), bf16),
            pltpu.VMEM((LOCAL_HEADS, NY, NC * NX, XROWS, COLS), bf16),
            pltpu.VMEM((ROWS_HERE, whole, COLS), bf16),
            pltpu.VMEM((ROWS_HERE, WIDTH_HERE, COLS), bf16),
            dma((2 * LOCAL_HEADS + 2,)),
            dma((6,)),
            dma((6,)),
            dma((LOCAL_HEADS,)),
            dma((LOCAL_HEADS,)),
            dma((LOCAL_HEADS, NX)),
            dma((LOCAL_HEADS, NX)),
            dma((LOCAL_HEADS, GROUPS)),
            dma((NZ,)),
            dma((NY,)),
            dma((NY,)),
            dma((NZ,)),
            dma((LOCAL_HEADS * GROUPS,)),
            dma((LOCAL_HEADS, NX)),
            dma((LOCAL_HEADS, NX)),
            dma((LOCAL_HEADS,)),
            dma((LOCAL_HEADS,)),
            dma((ROWS_HERE,)),
        ],
        compiler_params=pltpu.CompilerParams(
            collective_id=0, has_side_effects=True, vmem_limit_bytes=56 * 1024 * 1024
        ),
        cost_estimate=pl.CostEstimate(
            flops=3_000_000_000, bytes_accessed=5_000_000, transcendentals=2048
        ),
    )(queries, keys, values, w_out)


def solution(mesh):
    return jax.shard_map(
        per_device,
        mesh=mesh,
        in_specs=(
            P("depth", "head", None),
            P("depth", "head", None),
            P("depth", "head", None),
            P("head", None),
        ),
        out_specs=P("depth", "head", None),
        check_vma=False,
    )
```

```python
import math

import jax
import jax.numpy as jnp
from jax import lax
from jax.experimental import pallas as pl
from jax.experimental.pallas import tpu as pltpu
from jax.sharding import PartitionSpec as P

HEAD_DIM = 64
NZ, NX, NY, NC = 16, 4, 4, 2
LOCAL_HEADS = 3
ROWS_HERE = 12
WIDTH_HERE = LOCAL_HEADS * HEAD_DIM
COLS = 256
HALF = COLS // NC
XROWS = HALF // NX
GROUPS = XROWS // 8
HALF_SEQ = ROWS_HERE // 2
SCALING = 1.0 / math.sqrt(HEAD_DIM * ROWS_HERE * NZ * NX * NC)
MESH = pl.DeviceIdType.MESH


def exchange(
    q_hbm, k_hbm, v_hbm, w_hbm, att, w_v,
    q_v, k_v, vals, part, c_recv, csum, x_recv, xsum, z_recv, pg, zg, probs,
    load_sem, met_sem, v_ssem, v_rsem, c_ssem, c_rsem, x_ssem, x_rsem, z_ssem, z_rsem,
    zg_ssem, zg_rsem, z2_ssem, z2_rsem, xg_ssem, xg_rsem, cg_ssem, cg_rsem,
):
    me = lax.axis_index("depth")
    y = lax.axis_index("head")
    core = lax.rem(me, NC)
    x = lax.rem(me // NC, NX)
    z = me // (NC * NX)

    def at(z=z, x=x, core=core, y=y):
        return ((z * NX + x) * NC + core, y)

    def turn(index, by, size):
        return lax.rem(index + by, size)

    def remote(src, dst, ssem, rsem, device):
        return pltpu.make_async_remote_copy(
            src_ref=src, dst_ref=dst, send_sem=ssem, recv_sem=rsem,
            device_id=device, device_id_type=MESH,
        )

    def send(*args):
        copy = remote(*args)
        copy.start()
        return copy

    def arrived(dst, sem):
        remote(dst, dst, sem, sem, at()).wait_recv()

    mate = at(core=1 - core)
    barrier = pltpu.get_barrier_semaphore()
    near = (
        [at(y=turn(y, d, NY)) for d in range(1, NY)]
        + [mate]
        + [at(x=turn(x, d, NX)) for d in range(1, NX)]
    )
    for partner in near:
        pl.semaphore_signal(barrier, inc=1, device_id=partner, device_id_type=MESH)

    def along_z(semaphore, distance):
        @pl.when(z >= distance)
        def _():
            pl.semaphore_signal(
                semaphore, inc=1, device_id=at(z=z - distance), device_id_type=MESH
            )

        @pl.when(z + distance < NZ)
        def _():
            pl.semaphore_signal(
                semaphore, inc=1, device_id=at(z=z + distance), device_id_type=MESH
            )

    def count_z(distance):
        return jnp.where(z >= distance, 1, 0) + jnp.where(z + distance < NZ, 1, 0)

    along_z(barrier, 1)

    loads = []
    for h in range(LOCAL_HEADS):
        features = pl.ds(h * HEAD_DIM, HEAD_DIM)
        pair = (
            pltpu.make_async_copy(q_hbm.at[:, features, :], q_v.at[h], load_sem.at[2 * h]),
            pltpu.make_async_copy(k_hbm.at[:, features, :], k_v.at[h], load_sem.at[2 * h + 1]),
        )
        for copy in pair:
            copy.start()
        loads.append(pair)
    load_v = pltpu.make_async_copy(v_hbm, vals.at[y], load_sem.at[2 * LOCAL_HEADS])
    load_v.start()
    load_w = pltpu.make_async_copy(w_hbm, w_v, load_sem.at[2 * LOCAL_HEADS + 1])
    load_w.start()

    pl.semaphore_wait(barrier, len(near) + count_z(1))
    along_z(met_sem.at[0], 1)

    def meet(step):
        pl.semaphore_wait(met_sem.at[step], count_z(2**step))
        if step < 3:
            along_z(met_sem.at[step + 1], 2 ** (step + 1))

    started = []

    left, right, far = turn(y, NY - 1, NY), turn(y, 1, NY), turn(y, 2, NY)
    first, second = pl.ds(0, HALF_SEQ), pl.ds(HALF_SEQ, HALF_SEQ)

    def send_values(number, rows, target):
        started.append(send(
            v_hbm.at[rows], vals.at[y, rows], v_ssem.at[number], v_rsem.at[number], at(y=target)
        ))

    send_values(0, first, right)
    send_values(1, second, left)

    def second_hop():
        arrived(vals.at[left, first], v_rsem.at[0])
        send(vals.at[left, first], vals.at[left, first], v_ssem.at[4], v_rsem.at[4], at(y=right))
        arrived(vals.at[right, second], v_rsem.at[1])
        send(vals.at[right, second], vals.at[right, second], v_ssem.at[5], v_rsem.at[5], at(y=left))

    def second_hop_sent():
        for number, (slot, rows) in ((4, (left, first)), (5, (right, second))):
            remote(
                vals.at[slot, rows], vals.at[slot, rows], v_ssem.at[number], v_rsem.at[number], at(y=left)
            ).wait_send()

    theirs = pl.ds(pl.multiple_of((1 - core) * HALF, HALF), HALF)
    ours = pl.ds(pl.multiple_of(core * HALF, HALF), HALF)
    for h in range(LOCAL_HEADS):
        for copy in loads[h]:
            copy.wait()
        part[h] = lax.dot_general(
            q_v[h].reshape(ROWS_HERE * HEAD_DIM, COLS),
            k_v[h].reshape(ROWS_HERE * HEAD_DIM, COLS),
            (((0,), (0,)), ((), ())),
            preferred_element_type=jnp.float32,
        )
        started.append(send(part.at[h, theirs], c_recv.at[h], c_ssem.at[h], c_rsem.at[h], mate))
        if h == 0:
            meet(0)
    meet(1)

    for h in range(LOCAL_HEADS):
        arrived(c_recv.at[h], c_rsem.at[h])
        csum[h] = (part[h, ours, :] + c_recv[h]).reshape(NX, XROWS, COLS)
        for d in (2, 1, 3):
            other = turn(x, d, NX)
            started.append(send(
                csum.at[h, other], x_recv.at[h, x], x_ssem.at[h, d], x_rsem.at[h, x], at(x=other)
            ))
        if h == 0:
            send_values(2, second, right)
            send_values(3, first, left)
            meet(2)
    meet(3)


    def owner_of(h, t):
        return lax.rem(t * 4 + h + NZ - 2 * core, NZ)

    for h in range(LOCAL_HEADS):
        total = csum[h, x]
        for d in range(1, NX):
            other = turn(x, d, NX)
            arrived(x_recv.at[h, other], x_rsem.at[h, other])
            total = total + x_recv[h, other]
        xsum[h] = total.reshape(GROUPS, 8, COLS)
        for t in range(GROUPS):
            owner = owner_of(h, t)

            @pl.when(owner != z)
            def _():
                send(xsum.at[h, t], z_recv.at[z], z_ssem.at[h, t], z_rsem.at[z], at(z=owner))

            @pl.when(owner == z)
            def _():
                z_recv[z] = xsum[h, t]

    turned = turn(z, 2 * core, NZ)
    kind, group = lax.rem(turned, 4), turned // 4
    owns = kind < LOCAL_HEADS
    here = core * NX + x

    def same_kind():
        return [
            (dy, dz, at(y=turn(y, dy, NY), z=turn(z, 4 * dz, NZ)))
            for dz in (2, 1, 3, 0) for dy in (2, 1, 3, 0) if dy or dz
        ]

    def bundle_targets():
        return [at(z=turn(z, 1, NZ)), at(z=turn(z, NZ - 1, NZ)), at(z=lax.rem(z + NZ - 2 + 4 * core, NZ))]

    def send_x(h):
        return [
            send(
                probs.at[h, :, here], probs.at[h, :, here],
                xg_ssem.at[h, d], xg_rsem.at[h, x], at(x=turn(x, d, NX)),
            )
            for d in (2, 1, 3)
        ]

    @pl.when(owns)
    def _():
        for d in range(1, NZ):
            other = turn(z, d, NZ)
            arrived(z_recv.at[other], z_rsem.at[other])
        logits = jnp.sum(z_recv[...], axis=0) * SCALING
        top = jnp.max(logits, axis=-1, keepdims=True)
        powers = jnp.exp(logits - top)
        p = powers / jnp.sum(powers, axis=-1, keepdims=True)
        pg[...] = jnp.concatenate([p[:, :128], p[:, 128:]], axis=0).astype(jnp.bfloat16)
        zg[group, y] = pg[...]
        for dy, dz, device in same_kind():
            send(pg, zg.at[group, y], zg_ssem.at[dz, dy], zg_rsem.at[group, y], device)

    second_hop()

    @pl.when(owns)
    def _():
        for dy, dz, _ in same_kind():
            slot = (turn(group, dz, 4), turn(y, dy, NY))
            arrived(zg.at[slot], zg_rsem.at[slot])
        for other_y in range(NY):
            blocks = []
            for t in range(GROUPS):
                block = zg[t, other_y].astype(jnp.float32)
                blocks.append(jnp.concatenate([block[:8], block[8:]], axis=1))
            probs[kind, other_y, here] = jnp.concatenate(blocks, axis=0).astype(jnp.bfloat16)
        for number, device in enumerate(bundle_targets()):
            send(
                probs.at[kind, :, here], probs.at[kind, :, here],
                z2_ssem.at[number], z2_rsem.at[kind], device,
            )
        send_x(kind)

    for step in (1, 3, 2):
        h = lax.rem(kind + step, 4)

        @pl.when(h < LOCAL_HEADS)
        def _():
            arrived(probs.at[h, :, here], z2_rsem.at[h])
            send_x(h)

    our_blocks = pl.ds(pl.multiple_of(core * NX, NX), NX)
    mate_blocks = pl.ds(pl.multiple_of((1 - core) * NX, NX), NX)
    for step in (0, 1, 3, 2):
        h = lax.rem(kind + step, 4)

        @pl.when(h < LOCAL_HEADS)
        def _():
            for d in range(1, NX):
                other = turn(x, d, NX)
                arrived(probs.at[h, :, core * NX + other], xg_rsem.at[h, other])
            send(probs.at[h, :, our_blocks], probs.at[h, :, our_blocks], cg_ssem.at[h], cg_rsem.at[h], mate)

    load_v.wait()
    load_w.wait()
    arrived(vals.at[left, second], v_rsem.at[2])
    arrived(vals.at[right, first], v_rsem.at[3])
    arrived(vals.at[far, first], v_rsem.at[4])
    arrived(vals.at[far, second], v_rsem.at[5])
    for h in range(LOCAL_HEADS):
        arrived(probs.at[h, :, mate_blocks], cg_rsem.at[h])
        features = pl.ds(h * HEAD_DIM, HEAD_DIM)
        for other_y in range(NY):
            attended = lax.dot_general(
                vals[other_y, :, features, :].reshape(ROWS_HERE * HEAD_DIM, COLS),
                probs[h, other_y].reshape(COLS, COLS),
                (((1,), (1,)), ((), ())),
                preferred_element_type=jnp.float32,
            )
            att[:, pl.ds(other_y * WIDTH_HERE + h * HEAD_DIM, HEAD_DIM), :] = (
                attended.astype(jnp.bfloat16).reshape(ROWS_HERE, HEAD_DIM, COLS)
            )

    for copy in started:
        copy.wait_send()
    second_hop_sent()
    for h in range(LOCAL_HEADS):
        remote(
            probs.at[h, :, our_blocks], probs.at[h, :, our_blocks], cg_ssem.at[h], cg_rsem.at[h], mate
        ).wait_send()
        for d in range(1, NX):
            remote(
                probs.at[h, :, here], probs.at[h, :, here],
                xg_ssem.at[h, d], xg_rsem.at[h, x], at(x=turn(x, d, NX)),
            ).wait_send()
        for t in range(GROUPS):
            owner = owner_of(h, t)

            @pl.when(owner != z)
            def _():
                remote(
                    xsum.at[h, t], z_recv.at[z], z_ssem.at[h, t], z_rsem.at[z], at(z=owner)
                ).wait_send()

    @pl.when(owns)
    def _():
        for dy, dz, device in same_kind():
            remote(pg, zg.at[group, y], zg_ssem.at[dz, dy], zg_rsem.at[group, y], device).wait_send()
        for number, device in enumerate(bundle_targets()):
            remote(
                probs.at[kind, :, here], probs.at[kind, :, here],
                z2_ssem.at[number], z2_rsem.at[kind], device,
            ).wait_send()


def project(att, w_v, out_hbm, out_v, out_sem):
    copies = []
    for r in range(ROWS_HERE):
        out_v[r] = jnp.dot(w_v[...], att[r], preferred_element_type=jnp.float32).astype(jnp.bfloat16)
        copies.append(pltpu.make_async_copy(out_v.at[r], out_hbm.at[r], out_sem.at[r]))
        copies[-1].start()
    for copy in copies:
        copy.wait()


def per_device(queries, keys, values, w_out):
    f32, bf16 = jnp.float32, jnp.bfloat16
    dma = pltpu.SemaphoreType.DMA
    whole = WIDTH_HERE * NY
    any_spec = pl.BlockSpec(memory_space=pl.ANY)
    vmem_spec = pl.BlockSpec(memory_space=pltpu.VMEM)
    attended, weights = pl.pallas_call(
        exchange,
        out_shape=(
            pltpu.VMEM((ROWS_HERE, whole, COLS), bf16),
            pltpu.VMEM((WIDTH_HERE, whole), bf16),
        ),
        in_specs=[pl.BlockSpec(memory_space=pltpu.HBM)] * 4,
        out_specs=(vmem_spec, vmem_spec),
        scratch_shapes=[
            pltpu.VMEM((LOCAL_HEADS, ROWS_HERE, HEAD_DIM, COLS), bf16),
            pltpu.VMEM((LOCAL_HEADS, ROWS_HERE, HEAD_DIM, COLS), bf16),
            pltpu.VMEM((NY, ROWS_HERE, WIDTH_HERE, COLS), bf16),
            pltpu.VMEM((LOCAL_HEADS, COLS, COLS), f32),
            pltpu.VMEM((LOCAL_HEADS, HALF, COLS), f32),
            pltpu.VMEM((LOCAL_HEADS, NX, XROWS, COLS), f32),
            pltpu.VMEM((LOCAL_HEADS, NX, XROWS, COLS), f32),
            pltpu.VMEM((LOCAL_HEADS, GROUPS, 8, COLS), f32),
            pltpu.VMEM((NZ, 8, COLS), f32),
            pltpu.VMEM((16, 128), bf16),
            pltpu.VMEM((GROUPS, NY, 16, 128), bf16),
            pltpu.VMEM((LOCAL_HEADS, NY, NC * NX, XROWS, COLS), bf16),
            dma((2 * LOCAL_HEADS + 2,)),
            pltpu.SemaphoreType.REGULAR((4,)),
            dma((6,)),
            dma((6,)),
            dma((LOCAL_HEADS,)),
            dma((LOCAL_HEADS,)),
            dma((LOCAL_HEADS, NX)),
            dma((LOCAL_HEADS, NX)),
            dma((LOCAL_HEADS, GROUPS)),
            dma((NZ,)),
            dma((4, NY)),
            dma((GROUPS, NY)),
            dma((3,)),
            dma((LOCAL_HEADS,)),
            dma((LOCAL_HEADS, NX)),
            dma((LOCAL_HEADS, NX)),
            dma((LOCAL_HEADS,)),
            dma((LOCAL_HEADS,)),
        ],
        compiler_params=pltpu.CompilerParams(
            collective_id=0, has_side_effects=True, vmem_limit_bytes=58 * 1024 * 1024
        ),
        cost_estimate=pl.CostEstimate(
            flops=1_500_000_000, bytes_accessed=4_000_000, transcendentals=2048
        ),
    )(queries, keys, values, w_out)
    return pl.pallas_call(
        project,
        out_shape=jax.ShapeDtypeStruct(values.shape, bf16),
        in_specs=[vmem_spec, vmem_spec],
        out_specs=any_spec,
        scratch_shapes=[pltpu.VMEM((ROWS_HERE, WIDTH_HERE, COLS), bf16), dma((ROWS_HERE,))],
        compiler_params=pltpu.CompilerParams(vmem_limit_bytes=16 * 1024 * 1024),
        cost_estimate=pl.CostEstimate(
            flops=906_000_000, bytes_accessed=6_000_000, transcendentals=0
        ),
    )(attended, weights)


def solution(mesh):
    return jax.shard_map(
        per_device,
        mesh=mesh,
        in_specs=(
            P("depth", "head", None),
            P("depth", "head", None),
            P("depth", "head", None),
            P("head", None),
        ),
        out_specs=P("depth", "head", None),
        check_vma=False,
    )
```

```python
import math

import jax
import jax.numpy as jnp
from jax import lax
from jax.experimental import pallas as pl
from jax.experimental.pallas import tpu as pltpu
from jax.sharding import PartitionSpec as P

HEAD_DIM = 64
NZ, NX, NY, NC = 16, 4, 4, 2
LOCAL_HEADS = 3
ROWS_HERE = 12
WIDTH_HERE = LOCAL_HEADS * HEAD_DIM
COLS = 256
HALF = COLS // NC
XROWS = HALF // NX
OWNERS = 12
GROUPS = XROWS // 8
HALF_SEQ = ROWS_HERE // 2
SCALING = 1.0 / math.sqrt(HEAD_DIM * ROWS_HERE * NZ * NX * NC)
MESH = pl.DeviceIdType.MESH


def exchange(
    q_hbm, k_hbm, v_hbm, w_hbm, att, w_v,
    q_v, k_v, vals, part, c_recv, csum, x_recv, xsum, z_recv, pg, packed, probs,
    load_sem, met_sem, v_ssem, v_rsem, c_ssem, c_rsem, x_ssem, x_rsem, z_ssem, z_rsem,
    zg_ssem, zg_rsem, z2_ssem, z2_rsem, xg_ssem, xg_rsem, cg_ssem, cg_rsem,
):
    me = lax.axis_index("depth")
    y = lax.axis_index("head")
    core = lax.rem(me, NC)
    x = lax.rem(me // NC, NX)
    z = me // (NC * NX)

    def at(z=z, x=x, core=core, y=y):
        return ((z * NX + x) * NC + core, y)

    def turn(index, by, size):
        return lax.rem(index + by, size)

    def remote(src, dst, ssem, rsem, device):
        return pltpu.make_async_remote_copy(
            src_ref=src, dst_ref=dst, send_sem=ssem, recv_sem=rsem,
            device_id=device, device_id_type=MESH,
        )

    def send(*args):
        copy = remote(*args)
        copy.start()
        return copy

    def arrived(dst, sem):
        remote(dst, dst, sem, sem, at()).wait_recv()

    load_q = pltpu.make_async_copy(q_hbm, q_v, load_sem.at[0])
    load_k = pltpu.make_async_copy(k_hbm, k_v, load_sem.at[1])
    load_q.start()
    load_k.start()

    rank = jnp.where(z < 8, z, jnp.where(z < 12, z + 4, 23 - z))

    mate = at(core=1 - core)
    barrier = pltpu.get_barrier_semaphore()
    near = (
        [at(y=turn(y, d, NY)) for d in range(1, NY)]
        + [mate]
        + [at(x=turn(x, d, NX)) for d in range(1, NX)]
    )

    def signal(semaphore, device):
        pl.semaphore_signal(semaphore, inc=1, device_id=device, device_id_type=MESH)

    for partner in near:
        signal(barrier, partner)

    def signal_ranks(semaphore, start, stop):
        @pl.loop(start, stop)
        def _(other):
            signal(semaphore, at(z=jnp.where(other < 8, other, jnp.where(other < 12, 23 - other, other - 4))))

    signal_ranks(barrier, rank + 1, NZ)
    load_v = pltpu.make_async_copy(v_hbm, vals.at[y], load_sem.at[2])
    load_w = pltpu.make_async_copy(w_hbm, w_v, load_sem.at[3])

    started = []

    left, right, far = turn(y, NY - 1, NY), turn(y, 1, NY), turn(y, 2, NY)
    first, second = pl.ds(0, HALF_SEQ), pl.ds(HALF_SEQ, HALF_SEQ)

    def send_values(number, rows, target):
        started.append(send(
            v_hbm.at[rows], vals.at[y, rows], v_ssem.at[number], v_rsem.at[number], at(y=target)
        ))

    def second_hop():
        arrived(vals.at[left, first], v_rsem.at[0])
        send(vals.at[left, first], vals.at[left, first], v_ssem.at[4], v_rsem.at[4], at(y=right))
        arrived(vals.at[right, second], v_rsem.at[1])
        send(vals.at[right, second], vals.at[right, second], v_ssem.at[5], v_rsem.at[5], at(y=left))

    def second_hop_sent():
        for number, (slot, rows) in ((4, (left, first)), (5, (right, second))):
            remote(
                vals.at[slot, rows], vals.at[slot, rows], v_ssem.at[number], v_rsem.at[number], at(y=left)
            ).wait_send()

    theirs = pl.ds(pl.multiple_of((1 - core) * HALF, HALF), HALF)
    ours = pl.ds(pl.multiple_of(core * HALF, HALF), HALF)
    for h in range(LOCAL_HEADS):
        if h == 0:
            load_q.wait()
            load_k.wait()
        features = pl.ds(h * HEAD_DIM, HEAD_DIM)
        part[h] = lax.dot_general(
            q_v[:, features, :].reshape(ROWS_HERE * HEAD_DIM, COLS),
            k_v[:, features, :].reshape(ROWS_HERE * HEAD_DIM, COLS),
            (((0,), (0,)), ((), ())),
            preferred_element_type=jnp.float32,
        )
        if h == 0:
            pl.semaphore_wait(barrier, len(near) + rank)
        started.append(send(part.at[h, theirs], c_recv.at[h], c_ssem.at[h], c_rsem.at[h], mate))
        if h == 0:
            send_values(0, first, right)
            send_values(1, second, left)

    @pl.when(rank < OWNERS)
    def _():
        signal_ranks(met_sem, 0, rank)

    for h in range(LOCAL_HEADS):
        arrived(c_recv.at[h], c_rsem.at[h])
        csum[h] = (part[h, ours, :] + c_recv[h]).reshape(NX, XROWS, COLS)
        for d in (2, 1, 3):
            other = turn(x, d, NX)
            started.append(send(
                csum.at[h, other], x_recv.at[h, x], x_ssem.at[h, d], x_rsem.at[h, x], at(x=other)
            ))


    def owner_of(h, t):
        return lax.rem(20 - 4 * h + t, NZ)

    load_v.start()
    load_w.start()
    @pl.when(rank < OWNERS - 1)
    def _():
        pl.semaphore_wait(met_sem, OWNERS - 1 - rank)

    for h in range(LOCAL_HEADS):
        total = csum[h, x]
        for d in range(1, NX):
            other = turn(x, d, NX)
            arrived(x_recv.at[h, other], x_rsem.at[h, other])
            total = total + x_recv[h, other]
        xsum[h] = total.reshape(GROUPS, 8, COLS)
        for t in range(GROUPS):
            owner = owner_of(h, t)

            @pl.when(owner != z)
            def _():
                send(xsum.at[h, t], z_recv.at[z], z_ssem.at[h, t], z_rsem.at[z], at(z=owner))

            @pl.when(owner == z)
            def _():
                z_recv[z] = xsum[h, t]
    send_values(2, second, right)
    send_values(3, first, left)

    own_head, kind = lax.rem(NZ + 1 - z // 4, 4), lax.rem(z, 4)
    owns = own_head < LOCAL_HEADS
    here = core * NX + x

    def each_first(act):
        for number in (0, 1, 3, 2):
            other = 4 * number + kind
            for dy in (2, 1, 3):
                act(number, dy, at(y=turn(y, dy, NY), z=other))

            @pl.when(other != z)
            def _():
                act(number, 0, at(z=other))

    half, place = y // 2, lax.rem(y, 2)

    def first_copy(number, dy, device):
        return remote(
            pg, packed.at[half, here, kind, own_head, place],
            zg_ssem.at[number, dy], zg_rsem.at[own_head, y], device,
        )

    our_blocks = pl.ds(pl.multiple_of(core * NX, NX), NX)
    mate_blocks = pl.ds(pl.multiple_of((1 - core) * NX, NX), NX)

    def each_z(act):
        targets = (
            (turn(z, 1, NZ), z < NZ - 1),
            (turn(z, NZ - 1, NZ), z >= 0),
            (lax.rem(z + NZ - 2 + 4 * core, NZ), jnp.logical_or(core == 0, z < NZ - 2)),
            (0, z == 3),
            (jnp.maximum(z - 2, 0), jnp.logical_and(core == 1, z // 2 == 1)),
        )
        for number, (target, there) in enumerate(targets):
            @pl.when(there)
            def _():
                act(remote(
                    packed.at[:, here, kind], packed.at[:, here, kind],
                    z2_ssem.at[number], z2_rsem.at[kind], at(z=target),
                ))

    def x_copies(t):
        return [
            remote(
                packed.at[:, here, t], packed.at[:, here, t],
                xg_ssem.at[t, d], xg_rsem.at[t, x], at(x=turn(x, d, NX)),
            )
            for d in (2, 1, 3)
        ]

    def core_copy(t):
        return remote(
            packed.at[:, our_blocks, t], packed.at[:, our_blocks, t], cg_ssem.at[t], cg_rsem.at[t], mate
        )

    @pl.when(owns)
    def _():
        for d in range(1, NZ):
            other = turn(z, d, NZ)
            arrived(z_recv.at[other], z_rsem.at[other])
        logits = jnp.sum(z_recv[...], axis=0) * SCALING
        top = jnp.max(logits, axis=-1, keepdims=True)
        powers = jnp.exp(logits - top)
        p = powers / jnp.sum(powers, axis=-1, keepdims=True)
        pg[...] = jnp.concatenate([p[:, :128], p[:, 128:]], axis=0).astype(jnp.bfloat16)
        packed[half, here, kind, own_head, place] = pg[...]
        each_first(lambda *where: first_copy(*where).start())

    second_hop()

    for h in range(LOCAL_HEADS):
        for dy in range(1, NY):
            other = turn(y, dy, NY)
            arrived(packed.at[other // 2, here, kind, h, lax.rem(other, 2)], zg_rsem.at[h, other])

        @pl.when(own_head != h)
        def _():
            arrived(packed.at[half, here, kind, h, place], zg_rsem.at[h, y])

    def start(copies):
        for copy in copies:
            copy.start()

    others = [turn(kind, d, 4) for d in (1, 3, 2)]
    each_z(lambda copy: copy.start())
    start(x_copies(kind))
    for t in others:
        arrived(packed.at[:, here, t], z2_rsem.at[t])
        start(x_copies(t))
    for t in [kind] + others:
        for d in range(1, NX):
            other = turn(x, d, NX)
            arrived(packed.at[:, core * NX + other, t], xg_rsem.at[t, other])
        core_copy(t).start()

    def unpack(which):
        @pl.loop(0, LOCAL_HEADS * NY)
        def _(number):
            h, other_y = number // NY, lax.rem(number, NY)
            for b in range(NX):
                blocks = packed[other_y // 2, which * NX + b, :, h, lax.rem(other_y, 2)].astype(jnp.float32)
                probs[h, other_y, which * NX + b] = jnp.concatenate(
                    [blocks[:, :8].reshape(XROWS, 128), blocks[:, 8:].reshape(XROWS, 128)], axis=1
                ).astype(jnp.bfloat16)

    unpack(core)
    load_v.wait()
    load_w.wait()
    for copy in started:
        copy.wait_send()
    second_hop_sent()
    for h in range(LOCAL_HEADS):
        for t in range(GROUPS):
            owner = owner_of(h, t)

            @pl.when(owner != z)
            def _():
                remote(
                    xsum.at[h, t], z_recv.at[z], z_ssem.at[h, t], z_rsem.at[z], at(z=owner)
                ).wait_send()

    @pl.when(owns)
    def _():
        each_first(lambda *where: first_copy(*where).wait_send())

    each_z(lambda copy: copy.wait_send())
    for t in range(GROUPS):
        for copy in x_copies(t):
            copy.wait_send()
        core_copy(t).wait_send()
    arrived(vals.at[left, second], v_rsem.at[2])
    arrived(vals.at[right, first], v_rsem.at[3])
    arrived(vals.at[far, first], v_rsem.at[4])
    arrived(vals.at[far, second], v_rsem.at[5])
    for t in [kind] + others:
        arrived(packed.at[:, mate_blocks, t], cg_rsem.at[t])
    unpack(1 - core)
    for h in range(LOCAL_HEADS):
        features = pl.ds(h * HEAD_DIM, HEAD_DIM)
        for other_y in range(NY):
            attended = lax.dot_general(
                vals[other_y, :, features, :].reshape(ROWS_HERE * HEAD_DIM, COLS),
                probs[h, other_y].reshape(COLS, COLS),
                (((1,), (1,)), ((), ())),
                preferred_element_type=jnp.float32,
            )
            att[:, pl.ds(other_y * WIDTH_HERE + h * HEAD_DIM, HEAD_DIM), :] = (
                attended.astype(jnp.bfloat16).reshape(ROWS_HERE, HEAD_DIM, COLS)
            )


def project(att, w_v, out_hbm, out_v, out_sem):
    copies = []
    for r in range(ROWS_HERE):
        out_v[r] = jnp.dot(w_v[...], att[r], preferred_element_type=jnp.float32).astype(jnp.bfloat16)
        copies.append(pltpu.make_async_copy(out_v.at[r], out_hbm.at[r], out_sem.at[r]))
        copies[-1].start()
    for copy in copies:
        copy.wait()


def per_device(queries, keys, values, w_out):
    f32, bf16 = jnp.float32, jnp.bfloat16
    dma = pltpu.SemaphoreType.DMA
    whole = WIDTH_HERE * NY
    any_spec = pl.BlockSpec(memory_space=pl.ANY)
    vmem_spec = pl.BlockSpec(memory_space=pltpu.VMEM)
    attended, weights = pl.pallas_call(
        exchange,
        out_shape=(
            pltpu.VMEM((ROWS_HERE, whole, COLS), bf16),
            pltpu.VMEM((WIDTH_HERE, whole), bf16),
        ),
        in_specs=[pl.BlockSpec(memory_space=pltpu.HBM)] * 4,
        out_specs=(vmem_spec, vmem_spec),
        scratch_shapes=[
            pltpu.VMEM((ROWS_HERE, WIDTH_HERE, COLS), bf16),
            pltpu.VMEM((ROWS_HERE, WIDTH_HERE, COLS), bf16),
            pltpu.VMEM((NY, ROWS_HERE, WIDTH_HERE, COLS), bf16),
            pltpu.VMEM((LOCAL_HEADS, COLS, COLS), f32),
            pltpu.VMEM((LOCAL_HEADS, HALF, COLS), f32),
            pltpu.VMEM((LOCAL_HEADS, NX, XROWS, COLS), f32),
            pltpu.VMEM((LOCAL_HEADS, NX, XROWS, COLS), f32),
            pltpu.VMEM((LOCAL_HEADS, GROUPS, 8, COLS), f32),
            pltpu.VMEM((NZ, 8, COLS), f32),
            pltpu.VMEM((16, 128), bf16),
            pltpu.VMEM((2, NC * NX, GROUPS, LOCAL_HEADS, NY // 2, 16, 128), bf16),
            pltpu.VMEM((LOCAL_HEADS, NY, NC * NX, XROWS, COLS), bf16),
            dma((4,)),
            pltpu.SemaphoreType.REGULAR,
            dma((6,)),
            dma((6,)),
            dma((LOCAL_HEADS,)),
            dma((LOCAL_HEADS,)),
            dma((LOCAL_HEADS, NX)),
            dma((LOCAL_HEADS, NX)),
            dma((LOCAL_HEADS, GROUPS)),
            dma((NZ,)),
            dma((4, NY)),
            dma((LOCAL_HEADS, NY)),
            dma((5,)),
            dma((GROUPS,)),
            dma((GROUPS, NX)),
            dma((GROUPS, NX)),
            dma((GROUPS,)),
            dma((GROUPS,)),
        ],
        compiler_params=pltpu.CompilerParams(
            collective_id=0, has_side_effects=True, vmem_limit_bytes=58 * 1024 * 1024
        ),
        cost_estimate=pl.CostEstimate(
            flops=1_500_000_000, bytes_accessed=4_000_000, transcendentals=2048
        ),
    )(queries, keys, values, w_out)
    return pl.pallas_call(
        project,
        out_shape=jax.ShapeDtypeStruct(values.shape, bf16),
        in_specs=[vmem_spec, vmem_spec],
        out_specs=any_spec,
        scratch_shapes=[pltpu.VMEM((ROWS_HERE, WIDTH_HERE, COLS), bf16), dma((ROWS_HERE,))],
        compiler_params=pltpu.CompilerParams(vmem_limit_bytes=16 * 1024 * 1024),
        cost_estimate=pl.CostEstimate(
            flops=906_000_000, bytes_accessed=6_000_000, transcendentals=0
        ),
    )(attended, weights)


def solution(mesh):
    return jax.shard_map(
        per_device,
        mesh=mesh,
        in_specs=(
            P("depth", "head", None),
            P("depth", "head", None),
            P("depth", "head", None),
            P("head", None),
        ),
        out_specs=P("depth", "head", None),
        check_vma=False,
    )
```

```python
import math

import jax
import jax.numpy as jnp
from jax import lax
from jax.experimental import pallas as pl
from jax.experimental.pallas import tpu as pltpu
from jax.sharding import PartitionSpec as P

HEAD_DIM = 64
NZ, NX, NY, NC = 16, 4, 4, 2
LOCAL_HEADS = 3
ROWS_HERE = 12
WIDTH_HERE = LOCAL_HEADS * HEAD_DIM
COLS = 256
HALF = COLS // NC
XROWS = HALF // NX
OWNERS = 12
GROUPS = XROWS // 8
HALF_SEQ = ROWS_HERE // 2
SCALING = 1.0 / math.sqrt(HEAD_DIM * ROWS_HERE * NZ * NX * NC)
MESH = pl.DeviceIdType.MESH


def exchange(
    q_hbm, k_hbm, v_hbm, w_hbm, att, w_v,
    q_v, k_v, vals, part, c_recv, csum, x_recv, xsum, z_recv, pg, packed, probs,
    load_sem, met_sem, v_ssem, v_rsem, c_ssem, c_rsem, x_ssem, x_rsem, z_ssem, z_rsem,
    zg_ssem, zg_rsem, z2_ssem, z2_rsem, xg_ssem, xg_rsem, cg_ssem, cg_rsem,
):
    me = lax.axis_index("depth")
    y = lax.axis_index("head")
    core = lax.rem(me, NC)
    x = lax.rem(me // NC, NX)
    z = me // (NC * NX)

    def at(z=z, x=x, core=core, y=y):
        return ((z * NX + x) * NC + core, y)

    def turn(index, by, size):
        return lax.rem(index + by, size)

    def remote(src, dst, ssem, rsem, device):
        return pltpu.make_async_remote_copy(
            src_ref=src, dst_ref=dst, send_sem=ssem, recv_sem=rsem,
            device_id=device, device_id_type=MESH,
        )

    def send(*args):
        copy = remote(*args)
        copy.start()
        return copy

    def arrived(dst, sem):
        remote(dst, dst, sem, sem, at()).wait_recv()

    load_q = pltpu.make_async_copy(q_hbm, q_v, load_sem.at[0])
    load_k = pltpu.make_async_copy(k_hbm, k_v, load_sem.at[1])
    load_q.start()
    load_k.start()

    rank = jnp.where(z < 8, z, jnp.where(z < 12, z + 4, 23 - z))

    mate = at(core=1 - core)
    barrier = pltpu.get_barrier_semaphore()
    near = (
        [at(y=turn(y, d, NY)) for d in range(1, NY)]
        + [mate]
        + [at(x=turn(x, d, NX)) for d in range(1, NX)]
    )

    def signal(semaphore, device):
        pl.semaphore_signal(semaphore, inc=1, device_id=device, device_id_type=MESH)

    for partner in near:
        signal(barrier, partner)

    def z_of(other):
        return jnp.where(other < 8, other, jnp.where(other < 12, 23 - other, other - 4))

    def apart(a, b):
        za, zb = z_of(a), z_of(b)
        late = jnp.logical_and(a >= 8, za - zb > 4)
        mixed = jnp.logical_and(a // 2 == 3, jnp.logical_and(b >= 8, b < 11))
        return jnp.logical_or(late, mixed)

    def signal_ranks(semaphore, start, stop, far):
        @pl.loop(start, stop)
        def _(other):
            held_back = apart(jnp.minimum(rank, other), jnp.maximum(rank, other))

            @pl.when(held_back if far else jnp.logical_not(held_back))
            def _():
                signal(semaphore, at(z=z_of(other)))

    later = jnp.where(jnp.logical_and(z >= 8, z < 11), 11 - z, jnp.where(z >= 13, 2, 0))
    signal_ranks(barrier, rank + 1, NZ, False)
    load_v = pltpu.make_async_copy(v_hbm, vals.at[y], load_sem.at[2])
    load_w = pltpu.make_async_copy(w_hbm, w_v, load_sem.at[3])

    started = []

    left, right, far = turn(y, NY - 1, NY), turn(y, 1, NY), turn(y, 2, NY)
    first, second = pl.ds(0, HALF_SEQ), pl.ds(HALF_SEQ, HALF_SEQ)

    def send_values(number, rows, target):
        started.append(send(
            v_hbm.at[rows], vals.at[y, rows], v_ssem.at[number], v_rsem.at[number], at(y=target)
        ))

    def second_hop():
        arrived(vals.at[left, first], v_rsem.at[0])
        send(vals.at[left, first], vals.at[left, first], v_ssem.at[4], v_rsem.at[4], at(y=right))
        arrived(vals.at[right, second], v_rsem.at[1])
        send(vals.at[right, second], vals.at[right, second], v_ssem.at[5], v_rsem.at[5], at(y=left))

    def second_hop_sent():
        for number, (slot, rows) in ((4, (left, first)), (5, (right, second))):
            remote(
                vals.at[slot, rows], vals.at[slot, rows], v_ssem.at[number], v_rsem.at[number], at(y=left)
            ).wait_send()

    theirs = pl.ds(pl.multiple_of((1 - core) * HALF, HALF), HALF)
    ours = pl.ds(pl.multiple_of(core * HALF, HALF), HALF)
    for h in range(LOCAL_HEADS):
        if h == 0:
            load_q.wait()
            load_k.wait()
        features = pl.ds(h * HEAD_DIM, HEAD_DIM)
        part[h] = lax.dot_general(
            q_v[:, features, :].reshape(ROWS_HERE * HEAD_DIM, COLS),
            k_v[:, features, :].reshape(ROWS_HERE * HEAD_DIM, COLS),
            (((0,), (0,)), ((), ())),
            preferred_element_type=jnp.float32,
        )
        if h == 0:
            pl.semaphore_wait(barrier, len(near) + rank - later)
        started.append(send(part.at[h, theirs], c_recv.at[h], c_ssem.at[h], c_rsem.at[h], mate))
        if h == 0:
            send_values(0, first, right)
            send_values(1, second, left)

    @pl.when(rank < OWNERS)
    def _():
        signal_ranks(met_sem, 0, rank, False)

    @pl.when(z == 11)
    def _():
        for d in range(1, 4):
            signal(met_sem, at(z=z - d))

    for h in range(LOCAL_HEADS):
        arrived(c_recv.at[h], c_rsem.at[h])
        csum[h] = (part[h, ours, :] + c_recv[h]).reshape(NX, XROWS, COLS)
        for d in (2, 1, 3):
            other = turn(x, d, NX)
            started.append(send(
                csum.at[h, other], x_recv.at[h, x], x_ssem.at[h, d], x_rsem.at[h, x], at(x=other)
            ))


    def owner_of(h, t):
        return lax.rem(20 - 4 * h + t, NZ)

    load_v.start()
    load_w.start()


    @pl.when(rank < OWNERS - 1)
    def _():
        pl.semaphore_wait(met_sem, OWNERS - 1 - rank)

    @pl.when(z >= 13)
    def _():
        signal_ranks(met_sem, 6, 8, True)

    @pl.when(jnp.logical_and(rank >= OWNERS, rank < NZ - 1))
    def _():
        pl.semaphore_wait(met_sem, 1)

    for h in range(LOCAL_HEADS):
        total = csum[h, x]
        for d in range(1, NX):
            other = turn(x, d, NX)
            arrived(x_recv.at[h, other], x_rsem.at[h, other])
            total = total + x_recv[h, other]
        xsum[h] = total.reshape(GROUPS, 8, COLS)
        for t in range(GROUPS):
            owner = owner_of(h, t)

            @pl.when(owner != z)
            def _():
                send(xsum.at[h, t], z_recv.at[z], z_ssem.at[h, t], z_rsem.at[z], at(z=owner))

            @pl.when(owner == z)
            def _():
                z_recv[z] = xsum[h, t]
    send_values(2, second, right)
    send_values(3, first, left)

    own_head, kind = lax.rem(NZ + 1 - z // 4, 4), lax.rem(z, 4)
    owns = own_head < LOCAL_HEADS
    here = core * NX + x

    half, place = y // 2, lax.rem(y, 2)

    def each_first(act):
        def first_copy(number, dy, device, sem):
            act(remote(pg, packed.at[half, here, kind, own_head, place], zg_ssem.at[number, dy], sem, device))

        @pl.when(kind > 0)
        def _():
            for dy in range(NY):
                first_copy(4, dy, at(y=turn(y, dy, NY), z=0), z2_rsem.at[kind])

        for number in (0, 3, 1, 2):
            other = 4 * number + kind
            for dy in (2, 1, 3):
                first_copy(number, dy, at(y=turn(y, dy, NY), z=other), zg_rsem.at[own_head, y])

            @pl.when(other != z)
            def _():
                first_copy(number, 0, at(z=other), zg_rsem.at[own_head, y])

    our_blocks = pl.ds(pl.multiple_of(core * NX, NX), NX)
    mate_blocks = pl.ds(pl.multiple_of((1 - core) * NX, NX), NX)

    def each_z(act):
        targets = (
            (turn(z, 1, NZ), z < NZ - 1),
            (turn(z, NZ - 1, NZ), z != 1),
            (lax.rem(z + NZ - 2 + 4 * core, NZ), jnp.where(core == 0, z != 2, z < NZ - 2)),
            (1, jnp.logical_and(core == 1, z == 3)),
        )
        for number, (target, there) in enumerate(targets):
            @pl.when(there)
            def _():
                act(remote(
                    packed.at[:, here, kind], packed.at[:, here, kind],
                    z2_ssem.at[number], z2_rsem.at[kind], at(z=target),
                ))

    def x_copies(t):
        return [
            remote(
                packed.at[:, here, t], packed.at[:, here, t],
                xg_ssem.at[t, d], xg_rsem.at[t, x], at(x=turn(x, d, NX)),
            )
            for d in (2, 1, 3)
        ]

    def core_copy(t):
        return remote(
            packed.at[:, our_blocks, t], packed.at[:, our_blocks, t], cg_ssem.at[t], cg_rsem.at[t], mate
        )

    @pl.when(owns)
    def _():
        for d in range(1, NZ):
            other = turn(z, d, NZ)
            arrived(z_recv.at[other], z_rsem.at[other])
        logits = jnp.sum(z_recv[...], axis=0) * SCALING
        top = jnp.max(logits, axis=-1, keepdims=True)
        powers = jnp.exp(logits - top)
        p = powers / jnp.sum(powers, axis=-1, keepdims=True)
        pg[...] = jnp.concatenate([p[:, :128], p[:, 128:]], axis=0).astype(jnp.bfloat16)
        packed[half, here, kind, own_head, place] = pg[...]
        each_first(lambda copy: copy.start())

    second_hop()

    for h in range(LOCAL_HEADS):
        for dy in range(1, NY):
            other = turn(y, dy, NY)
            arrived(packed.at[other // 2, here, kind, h, lax.rem(other, 2)], zg_rsem.at[h, other])

        @pl.when(own_head != h)
        def _():
            arrived(packed.at[half, here, kind, h, place], zg_rsem.at[h, y])

    def start(copies):
        for copy in copies:
            copy.start()

    others = [turn(kind, jnp.where(z == 0, a, b), 4) for a, b in ((1, 3), (2, 1), (3, 2))]
    each_z(lambda copy: copy.start())
    start(x_copies(kind))
    for t in others:
        arrived(packed.at[:, here, t], z2_rsem.at[t])
        start(x_copies(t))
    for t in [kind] + others:
        for d in range(1, NX):
            other = turn(x, d, NX)
            arrived(packed.at[:, core * NX + other, t], xg_rsem.at[t, other])
        core_copy(t).start()

    def unpack(which):
        @pl.loop(0, LOCAL_HEADS * NY)
        def _(number):
            h, other_y = number // NY, lax.rem(number, NY)
            for b in range(NX):
                blocks = packed[other_y // 2, which * NX + b, :, h, lax.rem(other_y, 2)].astype(jnp.float32)
                probs[h, other_y, which * NX + b] = jnp.concatenate(
                    [blocks[:, :8].reshape(XROWS, 128), blocks[:, 8:].reshape(XROWS, 128)], axis=1
                ).astype(jnp.bfloat16)

    unpack(core)
    load_v.wait()
    load_w.wait()
    for copy in started:
        copy.wait_send()
    second_hop_sent()
    for h in range(LOCAL_HEADS):
        for t in range(GROUPS):
            owner = owner_of(h, t)

            @pl.when(owner != z)
            def _():
                remote(
                    xsum.at[h, t], z_recv.at[z], z_ssem.at[h, t], z_rsem.at[z], at(z=owner)
                ).wait_send()

    @pl.when(owns)
    def _():
        each_first(lambda copy: copy.wait_send())

    each_z(lambda copy: copy.wait_send())
    for t in range(GROUPS):
        for copy in x_copies(t):
            copy.wait_send()
        core_copy(t).wait_send()
    arrived(vals.at[left, second], v_rsem.at[2])
    arrived(vals.at[right, first], v_rsem.at[3])
    arrived(vals.at[far, first], v_rsem.at[4])
    arrived(vals.at[far, second], v_rsem.at[5])
    for t in [kind] + others:
        arrived(packed.at[:, mate_blocks, t], cg_rsem.at[t])
    unpack(1 - core)
    for h in range(LOCAL_HEADS):
        features = pl.ds(h * HEAD_DIM, HEAD_DIM)
        for other_y in range(NY):
            attended = lax.dot_general(
                vals[other_y, :, features, :].reshape(ROWS_HERE * HEAD_DIM, COLS),
                probs[h, other_y].reshape(COLS, COLS),
                (((1,), (1,)), ((), ())),
                preferred_element_type=jnp.float32,
            )
            att[:, pl.ds(other_y * WIDTH_HERE + h * HEAD_DIM, HEAD_DIM), :] = (
                attended.astype(jnp.bfloat16).reshape(ROWS_HERE, HEAD_DIM, COLS)
            )


def project(att, w_v, out_hbm, out_v, out_sem):
    copies = []
    for r in range(ROWS_HERE):
        out_v[r] = jnp.dot(w_v[...], att[r], preferred_element_type=jnp.float32).astype(jnp.bfloat16)
        copies.append(pltpu.make_async_copy(out_v.at[r], out_hbm.at[r], out_sem.at[r]))
        copies[-1].start()
    for copy in copies:
        copy.wait()


def per_device(queries, keys, values, w_out):
    f32, bf16 = jnp.float32, jnp.bfloat16
    dma = pltpu.SemaphoreType.DMA
    whole = WIDTH_HERE * NY
    any_spec = pl.BlockSpec(memory_space=pl.ANY)
    vmem_spec = pl.BlockSpec(memory_space=pltpu.VMEM)
    attended, weights = pl.pallas_call(
        exchange,
        out_shape=(
            pltpu.VMEM((ROWS_HERE, whole, COLS), bf16),
            pltpu.VMEM((WIDTH_HERE, whole), bf16),
        ),
        in_specs=[pl.BlockSpec(memory_space=pltpu.HBM)] * 4,
        out_specs=(vmem_spec, vmem_spec),
        scratch_shapes=[
            pltpu.VMEM((ROWS_HERE, WIDTH_HERE, COLS), bf16),
            pltpu.VMEM((ROWS_HERE, WIDTH_HERE, COLS), bf16),
            pltpu.VMEM((NY, ROWS_HERE, WIDTH_HERE, COLS), bf16),
            pltpu.VMEM((LOCAL_HEADS, COLS, COLS), f32),
            pltpu.VMEM((LOCAL_HEADS, HALF, COLS), f32),
            pltpu.VMEM((LOCAL_HEADS, NX, XROWS, COLS), f32),
            pltpu.VMEM((LOCAL_HEADS, NX, XROWS, COLS), f32),
            pltpu.VMEM((LOCAL_HEADS, GROUPS, 8, COLS), f32),
            pltpu.VMEM((NZ, 8, COLS), f32),
            pltpu.VMEM((16, 128), bf16),
            pltpu.VMEM((2, NC * NX, GROUPS, LOCAL_HEADS, NY // 2, 16, 128), bf16),
            pltpu.VMEM((LOCAL_HEADS, NY, NC * NX, XROWS, COLS), bf16),
            dma((4,)),
            pltpu.SemaphoreType.REGULAR,
            dma((6,)),
            dma((6,)),
            dma((LOCAL_HEADS,)),
            dma((LOCAL_HEADS,)),
            dma((LOCAL_HEADS, NX)),
            dma((LOCAL_HEADS, NX)),
            dma((LOCAL_HEADS, GROUPS)),
            dma((NZ,)),
            dma((5, NY)),
            dma((LOCAL_HEADS, NY)),
            dma((4,)),
            dma((GROUPS,)),
            dma((GROUPS, NX)),
            dma((GROUPS, NX)),
            dma((GROUPS,)),
            dma((GROUPS,)),
        ],
        compiler_params=pltpu.CompilerParams(
            collective_id=0, has_side_effects=True, vmem_limit_bytes=58 * 1024 * 1024
        ),
        cost_estimate=pl.CostEstimate(
            flops=1_500_000_000, bytes_accessed=4_000_000, transcendentals=2048
        ),
    )(queries, keys, values, w_out)
    return pl.pallas_call(
        project,
        out_shape=jax.ShapeDtypeStruct(values.shape, bf16),
        in_specs=[vmem_spec, vmem_spec],
        out_specs=any_spec,
        scratch_shapes=[pltpu.VMEM((ROWS_HERE, WIDTH_HERE, COLS), bf16), dma((ROWS_HERE,))],
        compiler_params=pltpu.CompilerParams(vmem_limit_bytes=16 * 1024 * 1024),
        cost_estimate=pl.CostEstimate(
            flops=906_000_000, bytes_accessed=6_000_000, transcendentals=0
        ),
    )(attended, weights)


def solution(mesh):
    return jax.shard_map(
        per_device,
        mesh=mesh,
        in_specs=(
            P("depth", "head", None),
            P("depth", "head", None),
            P("depth", "head", None),
            P("head", None),
        ),
        out_specs=P("depth", "head", None),
        check_vma=False,
    )
```

```python
import math

import jax
import jax.numpy as jnp
from jax import lax
from jax.experimental import pallas as pl
from jax.experimental.pallas import tpu as pltpu
from jax.sharding import PartitionSpec as P

HEAD_DIM = 64
NZ, NX, NY, NC = 16, 4, 4, 2
LOCAL_HEADS = 3
ROWS_HERE = 12
WIDTH_HERE = LOCAL_HEADS * HEAD_DIM
COLS = 256
HALF = COLS // NC
XROWS = HALF // NX
OWNERS = 12
GROUPS = XROWS // 8
HALF_SEQ = ROWS_HERE // 2
SCALING = 1.0 / math.sqrt(HEAD_DIM * ROWS_HERE * NZ * NX * NC)
MESH = pl.DeviceIdType.MESH


def exchange(
    q_hbm, k_hbm, v_hbm, w_hbm, att, w_v,
    q_v, k_v, vals, part, c_recv, csum, x_recv, xsum, z_recv, pg, packed, probs,
    load_sem, met_sem, v_ssem, v_rsem, c_ssem, c_rsem, x_ssem, x_rsem, z_ssem, z_rsem,
    zg_ssem, zg_rsem, z2_ssem, z2_rsem, xg_ssem, xg_rsem, cg_ssem, cg_rsem,
):
    me = lax.axis_index("depth")
    y = lax.axis_index("head")
    core = lax.rem(me, NC)
    x = lax.rem(me // NC, NX)
    z = me // (NC * NX)

    def at(z=z, x=x, core=core, y=y):
        return ((z * NX + x) * NC + core, y)

    def turn(index, by, size):
        return lax.rem(index + by, size)

    def remote(src, dst, ssem, rsem, device):
        return pltpu.make_async_remote_copy(
            src_ref=src, dst_ref=dst, send_sem=ssem, recv_sem=rsem,
            device_id=device, device_id_type=MESH,
        )

    def send(*args):
        copy = remote(*args)
        copy.start()
        return copy

    def arrived(dst, sem):
        remote(dst, dst, sem, sem, at()).wait_recv()

    load_q = pltpu.make_async_copy(q_hbm, q_v, load_sem.at[0])
    load_k = pltpu.make_async_copy(k_hbm, k_v, load_sem.at[1])
    load_q.start()
    load_k.start()

    rank = jnp.where(z < 8, z, jnp.where(z < 12, z + 4, 23 - z))

    mate = at(core=1 - core)
    barrier = pltpu.get_barrier_semaphore()
    near = (
        [at(y=turn(y, d, NY)) for d in range(1, NY)]
        + [mate]
        + [at(x=turn(x, d, NX)) for d in range(1, NX)]
    )

    def signal(semaphore, device):
        pl.semaphore_signal(semaphore, inc=1, device_id=device, device_id_type=MESH)

    for partner in near:
        signal(barrier, partner)

    def z_of(other):
        return jnp.where(other < 8, other, jnp.where(other < 12, 23 - other, other - 4))

    def apart(a, b):
        za, zb = z_of(a), z_of(b)
        late = jnp.logical_and(a >= 8, za - zb > 4)
        mixed = jnp.logical_and(a // 2 == 3, jnp.logical_and(b >= 8, b < 11))
        return jnp.logical_or(late, mixed)

    def signal_ranks(semaphore, start, stop, far):
        @pl.loop(start, stop)
        def _(other):
            held_back = apart(jnp.minimum(rank, other), jnp.maximum(rank, other))

            @pl.when(held_back if far else jnp.logical_not(held_back))
            def _():
                signal(semaphore, at(z=z_of(other)))

    later = jnp.where(jnp.logical_and(z >= 8, z < 11), 11 - z, jnp.where(z >= 13, 2, 0))
    signal_ranks(barrier, rank + 1, NZ, False)
    load_v = pltpu.make_async_copy(v_hbm, vals.at[y], load_sem.at[2])
    load_w = pltpu.make_async_copy(w_hbm, w_v, load_sem.at[3])

    started = []

    left, right, far = turn(y, NY - 1, NY), turn(y, 1, NY), turn(y, 2, NY)
    first, second = pl.ds(0, HALF_SEQ), pl.ds(HALF_SEQ, HALF_SEQ)

    def send_values(number, rows, target):
        started.append(send(
            v_hbm.at[rows], vals.at[y, rows], v_ssem.at[number], v_rsem.at[number], at(y=target)
        ))

    def second_hop():
        arrived(vals.at[left, first], v_rsem.at[0])
        send(vals.at[left, first], vals.at[left, first], v_ssem.at[4], v_rsem.at[4], at(y=right))
        arrived(vals.at[right, second], v_rsem.at[1])
        send(vals.at[right, second], vals.at[right, second], v_ssem.at[5], v_rsem.at[5], at(y=left))

    def second_hop_sent():
        for number, (slot, rows) in ((4, (left, first)), (5, (right, second))):
            remote(
                vals.at[slot, rows], vals.at[slot, rows], v_ssem.at[number], v_rsem.at[number], at(y=left)
            ).wait_send()

    theirs = pl.ds(pl.multiple_of((1 - core) * HALF, HALF), HALF)
    ours = pl.ds(pl.multiple_of(core * HALF, HALF), HALF)
    for h in range(LOCAL_HEADS):
        if h == 0:
            load_q.wait()
            load_k.wait()
        features = pl.ds(h * HEAD_DIM, HEAD_DIM)
        part[h] = lax.dot_general(
            q_v[:, features, :].reshape(ROWS_HERE * HEAD_DIM, COLS),
            k_v[:, features, :].reshape(ROWS_HERE * HEAD_DIM, COLS),
            (((0,), (0,)), ((), ())),
            preferred_element_type=jnp.float32,
        )
        if h == 0:
            pl.semaphore_wait(barrier, len(near) + rank - later)
        started.append(send(part.at[h, theirs], c_recv.at[h], c_ssem.at[h], c_rsem.at[h], mate))
        if h == 0:
            send_values(0, first, right)
            send_values(1, second, left)

    @pl.when(rank < OWNERS)
    def _():
        signal_ranks(met_sem, 0, rank, False)

    @pl.when(z == 11)
    def _():
        for d in range(1, 4):
            signal(met_sem, at(z=z - d))

    for h in range(LOCAL_HEADS):
        arrived(c_recv.at[h], c_rsem.at[h])
        csum[h] = (part[h, ours, :] + c_recv[h]).reshape(NX, XROWS, COLS)
        for d in (2, 1, 3):
            other = turn(x, d, NX)
            started.append(send(
                csum.at[h, other], x_recv.at[h, x], x_ssem.at[h, d], x_rsem.at[h, x], at(x=other)
            ))


    def owner_of(h, t):
        return lax.rem(20 - 4 * h + t, NZ)

    load_v.start()
    load_w.start()


    @pl.when(rank < OWNERS - 1)
    def _():
        pl.semaphore_wait(met_sem, OWNERS - 1 - rank)

    @pl.when(z >= 13)
    def _():
        signal_ranks(met_sem, 6, 8, True)

    @pl.when(jnp.logical_and(rank >= OWNERS, rank < NZ - 1))
    def _():
        pl.semaphore_wait(met_sem, 1)

    for h in range(LOCAL_HEADS):
        total = csum[h, x]
        for d in range(1, NX):
            other = turn(x, d, NX)
            arrived(x_recv.at[h, other], x_rsem.at[h, other])
            total = total + x_recv[h, other]
        xsum[h] = total.reshape(GROUPS, 8, COLS)
        for t in range(GROUPS):
            owner = owner_of(h, t)

            @pl.when(owner != z)
            def _():
                send(xsum.at[h, t], z_recv.at[z], z_ssem.at[h, t], z_rsem.at[z], at(z=owner))

            @pl.when(owner == z)
            def _():
                z_recv[z] = xsum[h, t]
    send_values(2, second, right)
    send_values(3, first, left)

    own_head, kind = lax.rem(NZ + 1 - z // 4, 4), lax.rem(z, 4)
    owns = own_head < LOCAL_HEADS
    here = core * NX + x

    half, place = y // 2, lax.rem(y, 2)

    def each_first(act):
        def first_copy(number, dy, device, sem):
            act(remote(pg, packed.at[half, here, kind, own_head, place], zg_ssem.at[number, dy], sem, device))

        @pl.when(kind > 0)
        def _():
            for dy in range(NY):
                first_copy(4, dy, at(y=turn(y, dy, NY), z=0), z2_rsem.at[kind])

        for number in (0, 3, 1, 2):
            other = 4 * number + kind
            for dy in (2, 1, 3):
                first_copy(number, dy, at(y=turn(y, dy, NY), z=other), zg_rsem.at[own_head, y])

            @pl.when(other != z)
            def _():
                first_copy(number, 0, at(z=other), zg_rsem.at[own_head, y])

    our_blocks = pl.ds(pl.multiple_of(core * NX, NX), NX)
    mate_blocks = pl.ds(pl.multiple_of((1 - core) * NX, NX), NX)

    def each_z(act):
        targets = (
            (turn(z, 1, NZ), z < NZ - 1),
            (turn(z, NZ - 1, NZ), z != 1),
            (lax.rem(z + NZ - 2 + 4 * core, NZ), jnp.where(core == 0, z != 2, z < NZ - 2)),
            (1, jnp.logical_and(core == 1, z == 3)),
        )
        for number, (target, there) in enumerate(targets):
            @pl.when(there)
            def _():
                act(remote(
                    packed.at[:, here, kind], packed.at[:, here, kind],
                    z2_ssem.at[number], z2_rsem.at[kind], at(z=target),
                ))

    def x_copies(t):
        return [
            remote(
                packed.at[:, here, t], packed.at[:, here, t],
                xg_ssem.at[t, d], xg_rsem.at[t, x], at(x=turn(x, d, NX)),
            )
            for d in (2, 1, 3)
        ]

    def core_copy(t):
        return remote(
            packed.at[:, our_blocks, t], packed.at[:, our_blocks, t], cg_ssem.at[t], cg_rsem.at[t], mate
        )

    @pl.when(owns)
    def _():
        for d in range(1, NZ):
            other = turn(z, d, NZ)
            arrived(z_recv.at[other], z_rsem.at[other])
        logits = jnp.sum(z_recv[...], axis=0) * SCALING
        top = jnp.max(logits, axis=-1, keepdims=True)
        powers = jnp.exp(logits - top)
        p = powers / jnp.sum(powers, axis=-1, keepdims=True)
        pg[...] = jnp.concatenate([p[:, :128], p[:, 128:]], axis=0).astype(jnp.bfloat16)
        packed[half, here, kind, own_head, place] = pg[...]
        each_first(lambda copy: copy.start())

    second_hop()

    for h in range(LOCAL_HEADS):
        for dy in range(1, NY):
            other = turn(y, dy, NY)
            arrived(packed.at[other // 2, here, kind, h, lax.rem(other, 2)], zg_rsem.at[h, other])

        @pl.when(own_head != h)
        def _():
            arrived(packed.at[half, here, kind, h, place], zg_rsem.at[h, y])

    def start(copies):
        for copy in copies:
            copy.start()

    others = [turn(kind, jnp.where(z == 0, a, b), 4) for a, b in ((1, 3), (2, 1), (3, 2))]
    each_z(lambda copy: copy.start())
    start(x_copies(kind))
    for t in others:
        arrived(packed.at[:, here, t], z2_rsem.at[t])
        start(x_copies(t))
    for t in [kind] + others:
        for d in range(1, NX):
            other = turn(x, d, NX)
            arrived(packed.at[:, core * NX + other, t], xg_rsem.at[t, other])
        core_copy(t).start()

    def unpack(which, h, other_y):
        for b in range(NX):
            blocks = packed[other_y // 2, which * NX + b, :, h, other_y % 2].astype(jnp.float32)
            probs[h, other_y, which * NX + b] = jnp.concatenate(
                [blocks[:, :8].reshape(XROWS, 128), blocks[:, 8:].reshape(XROWS, 128)], axis=1
            ).astype(jnp.bfloat16)

    for h in range(LOCAL_HEADS):
        for other_y in range(NY):
            unpack(core, h, other_y)
    load_v.wait()
    load_w.wait()
    for copy in started:
        copy.wait_send()
    second_hop_sent()
    for h in range(LOCAL_HEADS):
        for t in range(GROUPS):
            owner = owner_of(h, t)

            @pl.when(owner != z)
            def _():
                remote(
                    xsum.at[h, t], z_recv.at[z], z_ssem.at[h, t], z_rsem.at[z], at(z=owner)
                ).wait_send()

    @pl.when(owns)
    def _():
        each_first(lambda copy: copy.wait_send())

    each_z(lambda copy: copy.wait_send())
    for t in range(GROUPS):
        for copy in x_copies(t):
            copy.wait_send()
        core_copy(t).wait_send()
    arrived(vals.at[left, second], v_rsem.at[2])
    arrived(vals.at[right, first], v_rsem.at[3])
    arrived(vals.at[far, first], v_rsem.at[4])
    arrived(vals.at[far, second], v_rsem.at[5])
    for t in [kind] + others:
        arrived(packed.at[:, mate_blocks, t], cg_rsem.at[t])
    for h in range(LOCAL_HEADS):
        features = pl.ds(h * HEAD_DIM, HEAD_DIM)
        for other_y in range(NY):
            unpack(1 - core, h, other_y)
            attended = lax.dot_general(
                vals[other_y, :, features, :].reshape(ROWS_HERE * HEAD_DIM, COLS),
                probs[h, other_y].reshape(COLS, COLS),
                (((1,), (1,)), ((), ())),
                preferred_element_type=jnp.float32,
            )
            att[:, pl.ds(other_y * WIDTH_HERE + h * HEAD_DIM, HEAD_DIM), :] = (
                attended.astype(jnp.bfloat16).reshape(ROWS_HERE, HEAD_DIM, COLS)
            )


def project(att, w_v, out_hbm, out_v, out_sem):
    copies = []
    for r in range(ROWS_HERE):
        out_v[r] = jnp.dot(w_v[...], att[r], preferred_element_type=jnp.float32).astype(jnp.bfloat16)
        copies.append(pltpu.make_async_copy(out_v.at[r], out_hbm.at[r], out_sem.at[r]))
        copies[-1].start()
    for copy in copies:
        copy.wait()


def per_device(queries, keys, values, w_out):
    f32, bf16 = jnp.float32, jnp.bfloat16
    dma = pltpu.SemaphoreType.DMA
    whole = WIDTH_HERE * NY
    any_spec = pl.BlockSpec(memory_space=pl.ANY)
    vmem_spec = pl.BlockSpec(memory_space=pltpu.VMEM)
    attended, weights = pl.pallas_call(
        exchange,
        out_shape=(
            pltpu.VMEM((ROWS_HERE, whole, COLS), bf16),
            pltpu.VMEM((WIDTH_HERE, whole), bf16),
        ),
        in_specs=[pl.BlockSpec(memory_space=pltpu.HBM)] * 4,
        out_specs=(vmem_spec, vmem_spec),
        scratch_shapes=[
            pltpu.VMEM((ROWS_HERE, WIDTH_HERE, COLS), bf16),
            pltpu.VMEM((ROWS_HERE, WIDTH_HERE, COLS), bf16),
            pltpu.VMEM((NY, ROWS_HERE, WIDTH_HERE, COLS), bf16),
            pltpu.VMEM((LOCAL_HEADS, COLS, COLS), f32),
            pltpu.VMEM((LOCAL_HEADS, HALF, COLS), f32),
            pltpu.VMEM((LOCAL_HEADS, NX, XROWS, COLS), f32),
            pltpu.VMEM((LOCAL_HEADS, NX, XROWS, COLS), f32),
            pltpu.VMEM((LOCAL_HEADS, GROUPS, 8, COLS), f32),
            pltpu.VMEM((NZ, 8, COLS), f32),
            pltpu.VMEM((16, 128), bf16),
            pltpu.VMEM((2, NC * NX, GROUPS, LOCAL_HEADS, NY // 2, 16, 128), bf16),
            pltpu.VMEM((LOCAL_HEADS, NY, NC * NX, XROWS, COLS), bf16),
            dma((4,)),
            pltpu.SemaphoreType.REGULAR,
            dma((6,)),
            dma((6,)),
            dma((LOCAL_HEADS,)),
            dma((LOCAL_HEADS,)),
            dma((LOCAL_HEADS, NX)),
            dma((LOCAL_HEADS, NX)),
            dma((LOCAL_HEADS, GROUPS)),
            dma((NZ,)),
            dma((5, NY)),
            dma((LOCAL_HEADS, NY)),
            dma((4,)),
            dma((GROUPS,)),
            dma((GROUPS, NX)),
            dma((GROUPS, NX)),
            dma((GROUPS,)),
            dma((GROUPS,)),
        ],
        compiler_params=pltpu.CompilerParams(
            collective_id=0, has_side_effects=True, vmem_limit_bytes=58 * 1024 * 1024
        ),
        cost_estimate=pl.CostEstimate(
            flops=1_500_000_000, bytes_accessed=4_000_000, transcendentals=2048
        ),
    )(queries, keys, values, w_out)
    return pl.pallas_call(
        project,
        out_shape=jax.ShapeDtypeStruct(values.shape, bf16),
        in_specs=[vmem_spec, vmem_spec],
        out_specs=any_spec,
        scratch_shapes=[pltpu.VMEM((ROWS_HERE, WIDTH_HERE, COLS), bf16), dma((ROWS_HERE,))],
        compiler_params=pltpu.CompilerParams(vmem_limit_bytes=16 * 1024 * 1024),
        cost_estimate=pl.CostEstimate(
            flops=906_000_000, bytes_accessed=6_000_000, transcendentals=0
        ),
    )(attended, weights)


def solution(mesh):
    return jax.shard_map(
        per_device,
        mesh=mesh,
        in_specs=(
            P("depth", "head", None),
            P("depth", "head", None),
            P("depth", "head", None),
            P("head", None),
        ),
        out_specs=P("depth", "head", None),
        check_vma=False,
    )
```
